32 devices in a mesh: grp: 4 (over x, core), row: 4 (over z), col: 2 (over y).
Axes of the slice: x: 2, y: 2, z: 4, core: 2. Of those that a mesh axis runs over, the one named last changes fastest.
Arguments:
- block_rows: bfloat16 [8, 304, 10240], P('grp', None, ('row', 'col')), may hold values from -6 to 6
- inverse_factor: float32 [8, 304, 304], P('grp'), as said below
- live_rows: int32 [8], P('grp'), may hold values from 50 to 304, as said below
- shift: float32 [10240], P(('grp', 'row', 'col')), may hold values from 0.5 to 2
Outputs:
- factored: float32 [10240, 10240], P(('grp', 'row'), 'col')
The draws below stay inside these ranges and needn't reach their ends.
Inputs may be any that keep to these rules, and one draw needn't show every extreme that they name: `live_rows`: every block uses between 50 and 304 rows; some block uses exactly 304 and some exactly 50. `inverse_factor`: each block's matrix is lower triangular with a positive diagonal.
All inputs are finite; a program needn't handle non-finite values.
Results may differ from the reference program's by a relative error of at most 0.0043.
Values may be sent and summed in bfloat16 or wider, within the bound.
No kernel may reach another device: no remote copies, remote signals or barrier semaphores. Data moves between devices by JAX's collectives and lax.ppermute only.
A program may use at most 192 MiB of HBM per device.

```python
import math
import jax
import jax.numpy as jnp
from jax import lax

N = 10240
PW = 1024
PMAX = 304
PANELS = 1
BLOCKS = 8
NPAN = 10
SLAB = 64
TWIN = 32
N_GRP = 4
N_ROW = 4
N_COL = 2


def draw_inverse_factor(key, part):
    first_key, second_key = jax.random.split(jax.random.fold_in(key, 11))
    overall = 2.0 / math.sqrt(BLOCKS * PMAX)
    diagonal = jax.random.uniform(first_key, (BLOCKS, PMAX), jnp.float32, 0.5, 1.5)
    below = jax.random.normal(second_key, (BLOCKS, PMAX, PMAX), jnp.float32) * (0.4 / math.sqrt(PMAX))
    identity = jnp.eye(PMAX, dtype=jnp.float32)
    triangle = jnp.tril(below, -1) + diagonal[:, :, None] * identity[None, :, :]
    return (triangle * overall).astype(jnp.float32)


def draw_live_rows(key, part):
    first_key, second_key = jax.random.split(jax.random.fold_in(key, 23))
    counts = jax.random.randint(first_key, (BLOCKS,), PMAX // 6, PMAX + 1)
    spot = jax.random.randint(second_key, (), 0, BLOCKS)
    ordinal = jnp.arange(BLOCKS, dtype=jnp.int32)
    counts = jnp.where(ordinal == spot, PMAX, counts)
    counts = jnp.where(ordinal == (spot + 1) % BLOCKS, PMAX // 6, counts)
    return counts.astype(jnp.int32)


def block_levels(stream_key, shape, pieces, smallest, high):
    def one(dim, parts):
        heights = jax.random.uniform(jax.random.fold_in(jax.random.fold_in(stream_key, 6), dim), (parts,), jnp.float32, smallest / len(pieces), high / len(pieces))
        return jnp.repeat(jnp.exp(heights), shape[dim] // parts).reshape((-1,) + (1,) * (len(shape) - dim - 1))

    level = one(*pieces[0])
    for cut in pieces[1:]:
        level = level * one(*cut)
    return level


def scatter_about(stream_key, extent, width, limit, cuts=(), held_as=jnp.bfloat16):
    values = jax.random.normal(stream_key, extent, jnp.float32) * width
    if len(cuts) > 0:
        values = block_levels(stream_key, extent, cuts, -0.22, 0.18) * values
    return jnp.clip(values, min=-limit, max=limit).astype(held_as)


def setup_inputs(seed: int = 0) -> dict:
    splits = jax.random.split(jax.random.key(seed), 5)
    return {
        "block_rows": scatter_about(splits[0], (BLOCKS, PMAX, N), 1.0, 6.0, ((0, 4), (2, 8))),
        "inverse_factor": draw_inverse_factor(jax.random.fold_in(splits[4], 71), 0),
        "live_rows": draw_live_rows(jax.random.fold_in(splits[4], 71), 0),
        "shift": jnp.clip(0.5 + 1.5 * jax.random.uniform(splits[3], (N,), jnp.float32) ** block_levels(splits[3], (N,), ((0, 32),), -0.2, 0.2), 0.5, 2.0),
    }


def reference(block_rows, inverse_factor, live_rows, shift):
    highest = lax.Precision.HIGHEST
    ordinal = jnp.arange(PMAX, dtype=jnp.int32)
    live_mask = (ordinal[None, :] < live_rows[:, None]).astype(jnp.float32)
    masked_factor = inverse_factor * live_mask[:, :, None] * live_mask[:, None, :]
    natural_rows = block_rows.astype(jnp.float32).reshape(BLOCKS, PMAX, N_ROW, N_COL, N_GRP, NPAN, TWIN)
    natural_rows = jnp.transpose(natural_rows, (0, 1, 5, 4, 2, 3, 6)).reshape(BLOCKS, PMAX, N)
    whitened = jnp.einsum('bij,bjm->bim', masked_factor, natural_rows, precision=highest)
    whitened = whitened.astype(jnp.bfloat16).reshape(BLOCKS * PMAX, N)
    schur_sum = lax.dot_general(whitened.astype(jnp.float32), whitened.astype(jnp.float32), (((0,), (0,)), ((), ())), preferred_element_type=jnp.float32)
    shift_nat = jnp.transpose(shift.reshape(N_GRP, N_ROW, N_COL, NPAN, TWIN), (3, 0, 1, 2, 4)).reshape(N)
    matrix = schur_sum + jnp.diag(shift_nat)
    index = jnp.arange(N, dtype=jnp.int32)
    finished = []
    for panel in range(PANELS):
        first = panel * PW
        beyond = (panel + 1) * PW
        cholesky_factor = jnp.linalg.cholesky(matrix[first:beyond, first:beyond])
        solved = jax.scipy.linalg.solve_triangular(cholesky_factor, matrix[:, first:beyond].T, lower=True).T
        finished.append(jnp.where(index[:, None] >= index[None, first:beyond], solved, 0.0))
        trailing_part = solved[beyond:]
        update = jnp.dot(trailing_part.astype(jnp.float32), trailing_part.T.astype(jnp.float32), precision=highest, preferred_element_type=jnp.float32)
        matrix = matrix.at[beyond:, beyond:].add(-update)
    boundary = PANELS * PW
    trailing = jnp.where(index[:, None] >= boundary, matrix[:, boundary:], 0.0)
    whole = jnp.concatenate(finished + [trailing], axis=1)
    whole = whole.reshape(NPAN, N_GRP, N_ROW, SLAB, NPAN, N_GRP, N_ROW, N_COL, TWIN)
    whole = jnp.transpose(whole, (1, 2, 0, 3, 7, 4, 5, 6, 8))
    return whole.reshape(N, N)
```

```python
import functools

import jax
import jax.numpy as jnp
from jax import lax
from jax.experimental import pallas as pl
from jax.experimental.pallas import tpu as pltpu
from jax.sharding import PartitionSpec as P

PW = 1024
NPAN = 10
BASE = 128
LANES = 128
CHUNKS = ((1, 2, 3), (4, 5, 6), (7, 8, 9))

NN = (((1,), (0,)), ((), ()))
NT = (((1,), (1,)), ((), ()))
TN = (((0,), (0,)), ((), ()))


def dot1(a, b, dims=NN):
    return lax.dot_general(a, b, dims, preferred_element_type=jnp.float32)


def split(x):
    hi = x.astype(jnp.bfloat16)
    return hi, (x - hi.astype(jnp.float32)).astype(jnp.bfloat16)


def split_outside(x):
    hi = lax.reduce_precision(x, 8, 7)
    return hi.astype(jnp.bfloat16), (x - hi).astype(jnp.bfloat16)


def dot3(a, b, dims=NN, cut=split):
    a_hi, a_lo = cut(a)
    b_hi, b_lo = cut(b)
    return dot1(a_hi, b_hi, dims) + (dot1(a_hi, b_lo, dims) + dot1(a_lo, b_hi, dims))


def inverse_base(block):
    size = block.shape[0]
    height = 8
    rows = lax.broadcasted_iota(jnp.int32, (height, size), 0)
    r_id = lax.broadcasted_iota(jnp.int32, (size, size), 0)
    c_id = lax.broadcasted_iota(jnp.int32, (size, size), 1)
    left = block
    right = jnp.where(r_id == c_id, 1.0, 0.0).astype(jnp.float32)
    done = []
    for q in range(size // height):
        a = left[0:height]
        b = right[0:height]
        cols = [
            jnp.broadcast_to(a[:, q * height + k : q * height + k + 1], (height, size))
            for k in range(height)
        ]
        scale = jnp.zeros((height, size), jnp.float32)
        for j in range(height):
            root = lax.rsqrt(cols[j][j : j + 1])
            scale = jnp.where(rows == j, root, scale)
            if j + 1 < height:
                factor = jnp.where(rows > j, cols[j] * (root * root), 0.0)
                a = a - factor * a[j : j + 1]
                b = b - factor * b[j : j + 1]
                for k in range(j + 1, height):
                    cols[k] = cols[k] - factor * cols[k][j : j + 1]
        a = a * scale
        b = b * scale
        done.append(b)
        if (q + 1) * height < size:
            both = jnp.concatenate([a, b], axis=1)
            both_hi = both.astype(jnp.bfloat16).astype(jnp.float32)
            both_lo = both - both_hi
            lhs = jnp.concatenate([both_hi[:, :size], both_hi[:, :size], both_lo[:, :size]], axis=0)
            rhs = jnp.concatenate([both_hi, both_lo, both_hi], axis=0)
            update = dot1(lhs.astype(jnp.bfloat16), rhs.astype(jnp.bfloat16), TN)
            lo = (q + 1) * height
            left = left[height:] - update[lo:, :size]
            right = right[height:] - update[lo:, size:]
    return jnp.concatenate(done, axis=0)


def inverse_kernel(a_ref, out_ref, work):
    n = a_ref.shape[0]
    steps = n // BASE
    work[...] = a_ref[...]
    out_ref[...] = jnp.zeros_like(out_ref)
    for k in range(steps):
        lo, hi = k * BASE, (k + 1) * BASE
        inv = inverse_base(work[lo:hi, lo:hi])
        if k > 0:
            out_ref[lo:hi, 0:lo] = dot3(inv, out_ref[lo:hi, 0:lo])
        out_ref[lo:hi, lo:hi] = inv
        if k + 1 < steps:
            upper = dot3(inv, work[lo:hi, hi:])
            upper_t = upper.T
            t_hi, t_lo = split(upper_t)
            u_hi, u_lo = split(upper)
            work[hi:, hi:] -= dot1(t_hi, u_hi) + (dot1(t_hi, u_lo) + dot1(t_lo, u_hi))
            b_hi, b_lo = split(out_ref[lo:hi, 0:hi])
            out_ref[hi:, 0:hi] -= dot1(t_hi, b_hi) + (dot1(t_hi, b_lo) + dot1(t_lo, b_hi))


def cholesky_inverse(matrix):
    n = matrix.shape[0]
    return pl.pallas_call(
        inverse_kernel,
        out_shape=jax.ShapeDtypeStruct((n, n), jnp.float32),
        in_specs=[pl.BlockSpec(memory_space=pltpu.VMEM)],
        out_specs=pl.BlockSpec(memory_space=pltpu.VMEM),
        scratch_shapes=[pltpu.VMEM((n, n), jnp.float32)],
        compiler_params=pltpu.CompilerParams(vmem_limit_bytes=48 * 1024 * 1024),
        cost_estimate=pl.CostEstimate(
            flops=80_000_000_000, bytes_accessed=8 * n * n, transcendentals=n
        ),
        name="cholesky_inverse",
    )(matrix)


def trailing_kernel(meta, v_ref, w_ref, diag_ref, held_ref, out_ref):
    groups, rowcount, depth, lanes = w_ref.shape
    step = pl.program_id(0)
    rows = v_ref.shape[0]
    window = lanes // groups
    v = v_ref[...]
    wide = [w_ref[:, r].reshape(groups * depth, lanes) for r in range(rowcount)]
    parts = []
    for r in range(0, rowcount, 2):
        pair = dot1(v, jnp.concatenate([wide[r], wide[r + 1]], axis=1))
        parts += [pair[:, :lanes], pair[:, lanes:]]
    block = lax.broadcasted_iota(jnp.int32, (rows, lanes), 1) // window
    for bit in (1, 2):
        keep = (block & bit) == 0
        turned = list(parts)
        for low in range(rowcount):
            if low & bit:
                continue
            high = low | bit
            turned[low] = jnp.where(keep, parts[low], pltpu.roll(parts[high], bit * window, 1))
            turned[high] = jnp.where(
                keep, pltpu.roll(parts[low], lanes - bit * window, 1), parts[high]
            )
        parts = turned
    for g in range(groups):
        out_ref[:, g * lanes : (g + 1) * lanes] = parts[g]
    start = pl.multiple_of(meta[0] * 2 * window + step * 2 * window + meta[1] * window, window)
    out_ref[pl.ds(start, window), :] += diag_ref[0]


def trailing_block(v_t, gathered, diag, held, first, col_index):
    rows, depth = v_t.shape
    groups, rowcount, part, width = gathered.shape
    panels = width // LANES
    tile = rowcount * LANES
    meta = jnp.stack([jnp.int32(first), col_index.astype(jnp.int32)])
    return pl.pallas_call(
        trailing_kernel,
        out_shape=jax.ShapeDtypeStruct(held.shape, jnp.float32),
        grid_spec=pltpu.PrefetchScalarGridSpec(
            num_scalar_prefetch=1,
            grid=(panels,),
            in_specs=[
                pl.BlockSpec((rows, depth), lambda i, m: (0, 0)),
                pl.BlockSpec((groups, rowcount, part, LANES), lambda i, m: (0, 0, 0, i)),
                pl.BlockSpec((1,) + diag.shape[1:], lambda i, m: (i, 0, 0)),
                pl.BlockSpec(memory_space=pl.ANY),
            ],
            out_specs=pl.BlockSpec((rows, tile), lambda i, m: (0, first + i)),
        ),
        input_output_aliases={4: 0},
        compiler_params=pltpu.CompilerParams(vmem_limit_bytes=48 * 1024 * 1024),
        cost_estimate=pl.CostEstimate(
            flops=2 * rows * depth * tile * panels,
            bytes_accessed=depth * tile * panels * 2 + rows * tile * panels * 4,
            transcendentals=0,
        ),
        name="trailing_block",
    )(meta, v_t, gathered, diag, held)


def local(block_rows, inverse_factor, live_rows, shift):
    groups = lax.axis_size("grp")
    rowcount = lax.axis_size("row")
    colcount = lax.axis_size("col")
    owners = groups * rowcount
    slab = PW // owners
    window = slab // colcount
    col_index = lax.axis_index("col")
    own_owner = lax.axis_index("grp") * rowcount + lax.axis_index("row")
    blocks, padded, _ = block_rows.shape
    depth = blocks * padded
    local_rows = NPAN * slab
    lanes = groups * window
    everyone = ("grp", "row", "col")

    shift_panel = lax.all_gather(shift[:window], everyone, axis=0, tiled=True)

    ordinal = jnp.arange(padded, dtype=jnp.int32)
    live_mask = (ordinal[None, :] < live_rows[:, None]).astype(jnp.float32)
    masked_factor = inverse_factor * live_mask[:, :, None] * live_mask[:, None, :]
    turned_rows = jnp.transpose(
        block_rows.reshape(blocks, padded, groups, NPAN, window), (0, 1, 3, 2, 4)
    ).reshape(blocks, padded, NPAN * lanes)
    whitened = jnp.einsum(
        "bij,bjm->bim",
        masked_factor,
        turned_rows.astype(jnp.float32),
        precision=lax.Precision.HIGHEST,
    ).astype(jnp.bfloat16).reshape(depth, NPAN * lanes)

    panel_t = whitened[:, :lanes].T
    panel_all = lax.all_gather(panel_t, everyone, axis=0, tiled=False)
    panel_all = panel_all.reshape(groups, rowcount, colcount, groups, window, depth)
    panel_w = jnp.transpose(panel_all, (3, 1, 2, 4, 0, 5)).reshape(PW, groups * depth)

    pieces = jnp.transpose(
        whitened.T.reshape(NPAN, groups, window, depth), (1, 0, 2, 3)
    ).reshape(groups, NPAN * window, depth)
    pieces = lax.all_to_all(pieces, "grp", split_axis=0, concat_axis=0)
    rows_all = lax.all_gather(pieces, "col", axis=0, tiled=False)
    rows_all = rows_all.reshape(colcount, groups, NPAN, window, depth)
    rows_w = jnp.transpose(rows_all, (2, 0, 3, 1, 4)).reshape(local_rows, groups * depth)

    gathered = []
    for chunk in CHUNKS:
        part = whitened[:, chunk[0] * lanes : (chunk[-1] + 1) * lanes]
        whole = lax.all_gather(part, ("grp", "row"), axis=0, tiled=False)
        gathered.append(whole.reshape(groups, rowcount, depth, len(chunk) * lanes))

    panel_ids = jnp.arange(PW, dtype=jnp.int32)
    schur = dot1(panel_w, panel_w, NT)
    schur = schur + jnp.where(
        panel_ids[:, None] == panel_ids[None, :], shift_panel[None, :], 0.0
    )
    inverse = cholesky_inverse(schur)

    local_ids = jnp.arange(local_rows, dtype=jnp.int32)
    row_global = (local_ids // slab) * PW + own_owner * slab + local_ids % slab
    rows_schur = dot1(rows_w, panel_w, NT) + jnp.where(
        row_global[:, None] == panel_ids[None, :], shift_panel[None, :], 0.0
    )
    solved = dot3(rows_schur, inverse, NT, split_outside)
    factor_hi, factor_lo = split_outside(dot3(solved, inverse, NN, split_outside))
    reduced = rows_w.astype(jnp.float32) - (dot1(factor_hi, panel_w) + dot1(factor_lo, panel_w))
    v_t = jnp.where(local_ids[:, None] >= slab, reduced, 0.0).astype(jnp.bfloat16)

    panel_piece = lax.dynamic_index_in_dim(
        solved.reshape(local_rows, owners, colcount, window), col_index, 2, keepdims=False
    ).reshape(local_rows, owners * window)
    own_cols = jnp.arange(owners * window, dtype=jnp.int32)
    panel_cols = (own_cols // window) * slab + col_index * window + own_cols % window
    panel_piece = jnp.where(row_global[:, None] >= panel_cols[None, :], panel_piece, 0.0)

    tile = owners * window
    own_shift = shift.reshape(NPAN, window, 1)
    diag = jnp.where(
        own_cols[None, None, :]
        == own_owner * window + jnp.arange(window, dtype=jnp.int32)[None, :, None],
        own_shift,
        0.0,
    )
    if lanes == LANES and rowcount == groups == 4 and slab == 2 * window:
        out = jnp.zeros((local_rows, NPAN * tile), jnp.float32)
        out = lax.dynamic_update_slice(out, panel_piece, (0, 0))
        for chunk, whole in zip(CHUNKS, gathered):
            part = diag[chunk[0] : chunk[-1] + 1]
            out = trailing_block(v_t, whole, part, out, chunk[0], col_index)
        return out
    finished = [panel_piece]
    for chunk, whole in zip(CHUNKS, gathered):
        wide = whole.reshape(groups, rowcount, depth, len(chunk), groups, window)
        wide = jnp.transpose(wide, (0, 2, 3, 4, 1, 5)).reshape(groups * depth, len(chunk) * tile)
        product = dot1(v_t, wide).reshape(NPAN, slab, len(chunk), tile)
        for at, panel in enumerate(chunk):
            piece = product[:, :, at].reshape(local_rows, tile)
            spot = jnp.int32(panel * slab) + col_index * window
            old = lax.dynamic_slice(piece, (spot, jnp.int32(0)), (window, tile))
            finished.append(
                lax.dynamic_update_slice(piece, old + diag[panel], (spot, jnp.int32(0)))
            )
    return jnp.concatenate(finished, axis=1)


def solution(mesh):
    in_specs = (
        P("grp", None, ("row", "col")),
        P("grp", None, None),
        P("grp"),
        P(("grp", "row", "col")),
    )
    out_specs = P(("grp", "row"), "col")
    return jax.shard_map(local, mesh=mesh, in_specs=in_specs, out_specs=out_specs, check_vma=False)
```

```python
import functools

import jax
import jax.numpy as jnp
from jax import lax
from jax.experimental import pallas as pl
from jax.experimental.pallas import tpu as pltpu
from jax.sharding import PartitionSpec as P

PW = 1024
NPAN = 10
BASE = 128
LANES = 128
CHUNKS = (tuple(range(1, NPAN)),)

NN = (((1,), (0,)), ((), ()))
NT = (((1,), (1,)), ((), ()))
TN = (((0,), (0,)), ((), ()))


def dot1(a, b, dims=NN):
    return lax.dot_general(a, b, dims, preferred_element_type=jnp.float32)


def split(x):
    hi = x.astype(jnp.bfloat16)
    return hi, (x - hi.astype(jnp.float32)).astype(jnp.bfloat16)


def split_outside(x):
    hi = lax.reduce_precision(x, 8, 7)
    return hi.astype(jnp.bfloat16), (x - hi).astype(jnp.bfloat16)


def dot3(a, b, dims=NN, cut=split):
    a_hi, a_lo = cut(a)
    b_hi, b_lo = cut(b)
    return dot1(a_hi, b_hi, dims) + (dot1(a_hi, b_lo, dims) + dot1(a_lo, b_hi, dims))


def inverse_base(block):
    size = block.shape[0]
    height = 8
    rows = lax.broadcasted_iota(jnp.int32, (height, size), 0)
    r_id = lax.broadcasted_iota(jnp.int32, (size, size), 0)
    c_id = lax.broadcasted_iota(jnp.int32, (size, size), 1)
    left = block
    right = jnp.where(r_id == c_id, 1.0, 0.0).astype(jnp.float32)
    done = []
    for q in range(size // height):
        a = left[0:height]
        b = right[0:height]
        cols = [
            jnp.broadcast_to(a[:, q * height + k : q * height + k + 1], (height, size))
            for k in range(height)
        ]
        scale = jnp.zeros((height, size), jnp.float32)
        for j in range(height):
            root = lax.rsqrt(cols[j][j : j + 1])
            scale = jnp.where(rows == j, root, scale)
            if j + 1 < height:
                factor = jnp.where(rows > j, cols[j] * (root * root), 0.0)
                a = a - factor * a[j : j + 1]
                b = b - factor * b[j : j + 1]
                for k in range(j + 1, height):
                    cols[k] = cols[k] - factor * cols[k][j : j + 1]
        a = a * scale
        b = b * scale
        done.append(b)
        if (q + 1) * height < size:
            both = jnp.concatenate([a, b], axis=1)
            both_hi = both.astype(jnp.bfloat16).astype(jnp.float32)
            both_lo = both - both_hi
            lhs = jnp.concatenate([both_hi[:, :size], both_hi[:, :size], both_lo[:, :size]], axis=0)
            rhs = jnp.concatenate([both_hi, both_lo, both_hi], axis=0)
            update = dot1(lhs.astype(jnp.bfloat16), rhs.astype(jnp.bfloat16), TN)
            lo = (q + 1) * height
            left = left[height:] - update[lo:, :size]
            right = right[height:] - update[lo:, size:]
    return jnp.concatenate(done, axis=0)


def inverse_kernel(a_ref, out_ref, work):
    work[...] = a_ref[...]
    out_ref[...] = jnp.zeros_like(out_ref)
    invert(work, out_ref)


def invert(work, out_ref):
    n = work.shape[0]
    steps = n // BASE
    for k in range(steps):
        lo, hi = k * BASE, (k + 1) * BASE
        inv = inverse_base(work[lo:hi, lo:hi])
        if k > 0:
            out_ref[lo:hi, 0:lo] = dot3(inv, out_ref[lo:hi, 0:lo])
        out_ref[lo:hi, lo:hi] = inv
        if k + 1 < steps:
            upper = dot3(inv, work[lo:hi, hi:])
            upper_t = upper.T
            t_hi, t_lo = split(upper_t)
            u_hi, u_lo = split(upper)
            work[hi:, hi:] -= dot1(t_hi, u_hi) + (dot1(t_hi, u_lo) + dot1(t_lo, u_hi))
            b_hi, b_lo = split(out_ref[lo:hi, 0:hi])
            out_ref[hi:, 0:hi] -= dot1(t_hi, b_hi) + (dot1(t_hi, b_lo) + dot1(t_lo, b_hi))


def cholesky_inverse(matrix):
    n = matrix.shape[0]
    return pl.pallas_call(
        inverse_kernel,
        out_shape=jax.ShapeDtypeStruct((n, n), jnp.float32),
        in_specs=[pl.BlockSpec(memory_space=pltpu.VMEM)],
        out_specs=pl.BlockSpec(memory_space=pltpu.VMEM),
        scratch_shapes=[pltpu.VMEM((n, n), jnp.float32)],
        compiler_params=pltpu.CompilerParams(vmem_limit_bytes=48 * 1024 * 1024),
        cost_estimate=pl.CostEstimate(
            flops=80_000_000_000, bytes_accessed=8 * n * n, transcendentals=n
        ),
        name="cholesky_inverse",
    )(matrix)


def local_general(block_rows, inverse_factor, live_rows, shift):
    groups = lax.axis_size("grp")
    rowcount = lax.axis_size("row")
    colcount = lax.axis_size("col")
    owners = groups * rowcount
    slab = PW // owners
    window = slab // colcount
    col_index = lax.axis_index("col")
    own_owner = lax.axis_index("grp") * rowcount + lax.axis_index("row")
    blocks, padded, _ = block_rows.shape
    depth = blocks * padded
    local_rows = NPAN * slab
    lanes = groups * window
    everyone = ("grp", "row", "col")

    shift_panel = lax.all_gather(shift[:window], everyone, axis=0, tiled=True)

    ordinal = jnp.arange(padded, dtype=jnp.int32)
    live_mask = (ordinal[None, :] < live_rows[:, None]).astype(jnp.float32)
    masked_factor = inverse_factor * live_mask[:, :, None] * live_mask[:, None, :]
    turned_rows = jnp.transpose(
        block_rows.reshape(blocks, padded, groups, NPAN, window), (0, 1, 3, 2, 4)
    ).reshape(blocks, padded, NPAN * lanes)
    whitened = jnp.einsum(
        "bij,bjm->bim",
        masked_factor,
        turned_rows.astype(jnp.float32),
        precision=lax.Precision.HIGHEST,
    ).astype(jnp.bfloat16).reshape(depth, NPAN * lanes)

    panel_t = whitened[:, :lanes].T
    panel_all = lax.all_gather(panel_t, everyone, axis=0, tiled=False)
    panel_all = panel_all.reshape(groups, rowcount, colcount, groups, window, depth)
    panel_w = jnp.transpose(panel_all, (3, 1, 2, 4, 0, 5)).reshape(PW, groups * depth)

    pieces = jnp.transpose(
        whitened.T.reshape(NPAN, groups, window, depth), (1, 0, 2, 3)
    ).reshape(groups, NPAN * window, depth)
    pieces = lax.all_to_all(pieces, "grp", split_axis=0, concat_axis=0)
    rows_all = lax.all_gather(pieces, "col", axis=0, tiled=False)
    rows_all = rows_all.reshape(colcount, groups, NPAN, window, depth)
    rows_w = jnp.transpose(rows_all, (2, 0, 3, 1, 4)).reshape(local_rows, groups * depth)

    gathered = []
    for chunk in CHUNKS:
        part = whitened[:, chunk[0] * lanes : (chunk[-1] + 1) * lanes]
        whole = lax.all_gather(part, ("grp", "row"), axis=0, tiled=False)
        gathered.append(whole.reshape(groups, rowcount, depth, len(chunk) * lanes))

    panel_ids = jnp.arange(PW, dtype=jnp.int32)
    schur = dot1(panel_w, panel_w, NT)
    schur = schur + jnp.where(
        panel_ids[:, None] == panel_ids[None, :], shift_panel[None, :], 0.0
    )
    inverse = cholesky_inverse(schur)

    local_ids = jnp.arange(local_rows, dtype=jnp.int32)
    row_global = (local_ids // slab) * PW + own_owner * slab + local_ids % slab
    rows_schur = dot1(rows_w, panel_w, NT) + jnp.where(
        row_global[:, None] == panel_ids[None, :], shift_panel[None, :], 0.0
    )
    solved = dot3(rows_schur, inverse, NT, split_outside)
    factor_hi, factor_lo = split_outside(dot3(solved, inverse, NN, split_outside))
    reduced = rows_w.astype(jnp.float32) - (dot1(factor_hi, panel_w) + dot1(factor_lo, panel_w))
    v_t = jnp.where(local_ids[:, None] >= slab, reduced, 0.0).astype(jnp.bfloat16)

    panel_piece = lax.dynamic_index_in_dim(
        solved.reshape(local_rows, owners, colcount, window), col_index, 2, keepdims=False
    ).reshape(local_rows, owners * window)
    own_cols = jnp.arange(owners * window, dtype=jnp.int32)
    panel_cols = (own_cols // window) * slab + col_index * window + own_cols % window
    panel_piece = jnp.where(row_global[:, None] >= panel_cols[None, :], panel_piece, 0.0)

    tile = owners * window
    own_shift = shift.reshape(NPAN, window, 1)
    diag = jnp.where(
        own_cols[None, None, :]
        == own_owner * window + jnp.arange(window, dtype=jnp.int32)[None, :, None],
        own_shift,
        0.0,
    )
    finished = [panel_piece]
    for chunk, whole in zip(CHUNKS, gathered):
        wide = whole.reshape(groups, rowcount, depth, len(chunk), groups, window)
        wide = jnp.transpose(wide, (0, 2, 3, 4, 1, 5)).reshape(groups * depth, len(chunk) * tile)
        product = dot1(v_t, wide).reshape(NPAN, slab, len(chunk), tile)
        for at, panel in enumerate(chunk):
            piece = product[:, :, at].reshape(local_rows, tile)
            spot = jnp.int32(panel * slab) + col_index * window
            old = lax.dynamic_slice(piece, (spot, jnp.int32(0)), (window, tile))
            finished.append(
                lax.dynamic_update_slice(piece, old + diag[panel], (spot, jnp.int32(0)))
            )
    return jnp.concatenate(finished, axis=1)


def swap(x, axis, bits):
    count = lax.axis_size(axis)
    return lax.ppermute(x, axis, [(i, i ^ bits) for i in range(count)])


def turn(x, axis, by):
    count = lax.axis_size(axis)
    return lax.ppermute(x, axis, [(i, (i + by) % count) for i in range(count)])


def spare_sum(tile, first):
    lane = lax.broadcasted_iota(jnp.int32, tile.shape, 1)
    return jnp.sum(
        jnp.where(lane >= first, tile.astype(jnp.float32), 0.0), axis=1, keepdims=True
    )


def panel_kernel(depth, place, *refs):
    pieces, (panel_ref, out_ref, work) = refs[:-3], refs[-3:]
    own_g, own_r, own_c = place[0], place[1], place[2]
    wide = panel_ref.shape[1] // 4
    half = pieces[0].shape[1]
    window = half // 2

    def lay(piece, top, core_bit, x_bit, y_bit, z_step):
        dg = own_g ^ (core_bit + 2 * x_bit)
        r = (own_r + 4 - z_step) % 4
        c = own_c ^ y_bit
        lane = pl.multiple_of(dg * wide, LANES)
        for g in range(2):
            row = ((top * 2 + g) * 4 + r) * 2 * window + c * window
            panel_ref[pl.ds(pl.multiple_of(row, window), window), pl.ds(lane, wide)] = piece[
                g * window : (g + 1) * window, :
            ]

    at = 0
    for core_bit in range(2):
        for z_step in range(4):
            for y_bit in range(2):
                for x_bit in range(2):
                    lay(pieces[at][y_bit * 2 + x_bit], 0, core_bit, x_bit, y_bit, z_step)
            at += 1
    for core_bit in range(2):
        for x_bit in range(2):
            for y_bit in range(2):
                for z_step in range(4):
                    lay(pieces[at][y_bit * 4 + z_step], 1, core_bit, x_bit, y_bit, z_step)
            at += 1

    n = work.shape[0]
    steps = n // BASE
    cut = depth % LANES
    lane = lax.broadcasted_iota(jnp.int32, (BASE, LANES), 1)
    on_diagonal = lax.broadcasted_iota(jnp.int32, (BASE, BASE), 0) == lax.broadcasted_iota(
        jnp.int32, (BASE, BASE), 1
    )
    for k in range(steps):
        lo, hi = k * BASE, (k + 1) * BASE
        total = jnp.zeros((BASE, n - lo), jnp.float32)
        moved = jnp.zeros((BASE, 1), jnp.float32)
        for dg in range(4):
            start = dg * wide
            last = panel_ref[lo:hi, start + wide - LANES : start + wide]
            moved = moved + spare_sum(last, cut)
            kept = jnp.where(lane < cut, last.astype(jnp.float32), 0.0).astype(jnp.bfloat16)
            mine = jnp.concatenate(
                [panel_ref[lo:hi, start : start + wide - LANES], kept], axis=1
            )
            total = total + dot1(mine, panel_ref[lo:, start : start + wide], NT)
        work[lo:hi, lo:] = total
        work[lo:hi, lo:hi] += jnp.where(on_diagonal, moved, 0.0)

    out_ref[...] = jnp.zeros_like(out_ref)
    invert(work, out_ref)


def panel_inverse(place, pieces, depth):
    wide = pieces[0].shape[-1]
    return pl.pallas_call(
        functools.partial(panel_kernel, depth),
        out_shape=(
            jax.ShapeDtypeStruct((PW, 4 * wide), jnp.bfloat16),
            jax.ShapeDtypeStruct((PW, PW), jnp.float32),
        ),
        in_specs=[pl.BlockSpec(memory_space=pltpu.SMEM)]
        + [pl.BlockSpec(memory_space=pltpu.VMEM)] * len(pieces),
        out_specs=(
            pl.BlockSpec(memory_space=pltpu.VMEM),
            pl.BlockSpec(memory_space=pltpu.VMEM),
        ),
        scratch_shapes=[pltpu.VMEM((PW, PW), jnp.float32)],
        compiler_params=pltpu.CompilerParams(vmem_limit_bytes=48 * 1024 * 1024),
        cost_estimate=pl.CostEstimate(
            flops=60_000_000_000, bytes_accessed=16 * 1024 * 1024, transcendentals=PW
        ),
        name="panel_inverse",
    )(place, *pieces)


def rows_kernel(depth, place, panel_ref, inv_ref, *refs):
    pieces, (first_ref, v_ref, rows_w, solved) = refs[:-4], refs[-4:]
    own_g, own_r, own_c = place[0], place[1], place[2]
    owner = own_g * 4 + own_r
    rows, total = rows_w.shape
    wide = total // 4
    slab = rows // NPAN
    window = slab // 2
    for y_bit in range(2):
        c = own_c ^ y_bit
        for step in range(4):
            lane = pl.multiple_of((own_g ^ step) * wide, LANES)
            piece = pieces[y_bit * 4 + step]
            for p in range(NPAN):
                row = pl.multiple_of(p * slab + c * window, window)
                rows_w[pl.ds(row, window), pl.ds(lane, wide)] = piece[
                    p * window : (p + 1) * window, :
                ]

    n = panel_ref.shape[0]
    schur = dot1(rows_w[...], panel_ref[...], NT)
    start = pl.multiple_of(owner * slab, slab)
    moved = jnp.zeros((slab, 1), jnp.float32)
    for dg in range(4):
        last = panel_ref[pl.ds(start, slab), (dg + 1) * wide - LANES : (dg + 1) * wide]
        moved = moved + spare_sum(last, depth % LANES)
    row_id = lax.broadcasted_iota(jnp.int32, (slab, n), 0)
    col_id = lax.broadcasted_iota(jnp.int32, (slab, n), 1)
    top = schur[:slab] + jnp.where(col_id == row_id + start, moved, 0.0)
    schur = jnp.concatenate([top, schur[slab:]], axis=0)

    inv_hi, inv_lo = split(inv_ref[...])
    s_hi, s_lo = split(schur)
    y = dot1(s_hi, inv_hi, NT) + (dot1(s_hi, inv_lo, NT) + dot1(s_lo, inv_hi, NT))
    solved[...] = y
    y_hi, y_lo = split(y)
    z = dot1(y_hi, inv_hi) + (dot1(y_hi, inv_lo) + dot1(y_lo, inv_hi))
    z_hi, z_lo = split(z)
    live = lax.broadcasted_iota(jnp.int32, (rows, wide), 0) >= slab
    parts = []
    for dg in range(4):
        own = panel_ref[:, dg * wide : (dg + 1) * wide]
        part = rows_w[:, dg * wide : (dg + 1) * wide].astype(jnp.float32) - (
            dot1(z_hi, own) + dot1(z_lo, own)
        )
        parts.append(jnp.where(live, part, 0.0)[:, :depth])
    v_ref[...] = jnp.concatenate(parts, axis=1).astype(jnp.bfloat16)

    lane = lax.broadcasted_iota(jnp.int32, (rows, LANES), 1)
    row = lax.broadcasted_iota(jnp.int32, (rows, LANES), 0)
    own_row = row // slab * PW + start + row % slab
    quarter = lane // window
    for at in range(n // 2 // LANES):
        low = solved[:, 2 * at * LANES : (2 * at + 1) * LANES]
        high = solved[:, (2 * at + 1) * LANES : (2 * at + 2) * LANES]
        back = (LANES - own_c * window) % LANES
        low = pltpu.roll(low, back, 1)
        high = pltpu.roll(high, back, 1)
        piece = jnp.where(
            quarter == 0,
            low,
            jnp.where(
                quarter == 1,
                pltpu.roll(low, LANES - window, 1),
                jnp.where(
                    quarter == 2,
                    pltpu.roll(high, 2 * window, 1),
                    pltpu.roll(high, window, 1),
                ),
            ),
        )
        own_col = (at * 4 + quarter) * slab + own_c * window + lane % window
        first_ref[:, at * LANES : (at + 1) * LANES] = jnp.where(own_row >= own_col, piece, 0.0)


def rows_update(place, panel, inverse, pieces, depth, rows):
    total = panel.shape[1]
    return pl.pallas_call(
        functools.partial(rows_kernel, depth),
        out_shape=(
            jax.ShapeDtypeStruct((rows, PW // 2), jnp.float32),
            jax.ShapeDtypeStruct((rows, 4 * depth), jnp.bfloat16),
        ),
        in_specs=[pl.BlockSpec(memory_space=pltpu.SMEM)]
        + [pl.BlockSpec(memory_space=pltpu.VMEM)] * (2 + len(pieces)),
        out_specs=(
            pl.BlockSpec(memory_space=pltpu.VMEM),
            pl.BlockSpec(memory_space=pltpu.VMEM),
        ),
        scratch_shapes=[
            pltpu.VMEM((rows, total), jnp.bfloat16),
            pltpu.VMEM((rows, PW), jnp.float32),
        ],
        compiler_params=pltpu.CompilerParams(vmem_limit_bytes=56 * 1024 * 1024),
        cost_estimate=pl.CostEstimate(
            flops=16_000_000_000, bytes_accessed=16 * 1024 * 1024, transcendentals=0
        ),
        name="rows_update",
    )(place, panel, inverse, *pieces)


def trailing_kernel(place, v_ref, first_ref, w_ref, diag_ref, out_ref):
    step = pl.program_id(0)

    @pl.when(step == 0)
    def _():
        out_ref[...] = first_ref[...]

    @pl.when(step > 0)
    def _():
        groups, rowcount, depth, lanes = w_ref.shape
        rows = v_ref.shape[0]
        window = lanes // groups
        v = v_ref[...]
        wide = [w_ref[:, r].reshape(groups * depth, lanes) for r in range(rowcount)]
        parts = []
        for r in range(0, rowcount, 2):
            pair = dot1(v, jnp.concatenate([wide[r], wide[r + 1]], axis=1))
            parts += [pair[:, :lanes], pair[:, lanes:]]
        block = lax.broadcasted_iota(jnp.int32, (rows, lanes), 1) // window
        for bit in (1, 2):
            keep = (block & bit) == 0
            turned = list(parts)
            for low in range(rowcount):
                if low & bit:
                    continue
                high = low | bit
                turned[low] = jnp.where(
                    keep, parts[low], pltpu.roll(parts[high], bit * window, 1)
                )
                turned[high] = jnp.where(
                    keep, pltpu.roll(parts[low], lanes - bit * window, 1), parts[high]
                )
            parts = turned
        for g in range(groups):
            out_ref[:, g * lanes : (g + 1) * lanes] = parts[g]
        start = pl.multiple_of(step * 2 * window + place[2] * window, window)
        out_ref[pl.ds(start, window), :] += diag_ref[0]


def trailing(place, v_t, first, gathered, diag):
    rows, depth = v_t.shape
    groups, rowcount, part, width = gathered.shape
    tile = rowcount * LANES
    return pl.pallas_call(
        trailing_kernel,
        out_shape=jax.ShapeDtypeStruct((rows, NPAN * tile), jnp.float32),
        grid_spec=pltpu.PrefetchScalarGridSpec(
            num_scalar_prefetch=1,
            grid=(NPAN,),
            in_specs=[
                pl.BlockSpec((rows, depth), lambda i, m: (0, 0)),
                pl.BlockSpec((rows, tile), lambda i, m: (0, 0)),
                pl.BlockSpec(
                    (groups, rowcount, part, LANES),
                    lambda i, m: (0, 0, 0, jnp.maximum(i - 1, 0)),
                ),
                pl.BlockSpec((1,) + diag.shape[1:], lambda i, m: (i, 0, 0)),
            ],
            out_specs=pl.BlockSpec((rows, tile), lambda i, m: (0, i)),
        ),
        compiler_params=pltpu.CompilerParams(vmem_limit_bytes=56 * 1024 * 1024),
        cost_estimate=pl.CostEstimate(
            flops=2 * rows * depth * tile * NPAN,
            bytes_accessed=depth * tile * NPAN * 2 + rows * tile * NPAN * 4,
            transcendentals=0,
        ),
        name="trailing",
    )(place, v_t, first, gathered, diag)


def local(block_rows, inverse_factor, live_rows, shift):
    groups = lax.axis_size("grp")
    rowcount = lax.axis_size("row")
    colcount = lax.axis_size("col")
    owners = groups * rowcount
    window = PW // owners // colcount
    lanes = groups * window
    if lanes != LANES or groups != 4 or rowcount != 4 or colcount != 2:
        return local_general(block_rows, inverse_factor, live_rows, shift)
    own_g = lax.axis_index("grp").astype(jnp.int32)
    own_r = lax.axis_index("row").astype(jnp.int32)
    own_c = lax.axis_index("col").astype(jnp.int32)
    place = jnp.stack([own_g, own_r, own_c])
    blocks, padded, _ = block_rows.shape
    depth = blocks * padded
    wide = -(-(depth + 3) // LANES) * LANES
    local_rows = NPAN * PW // owners

    ordinal = jnp.arange(padded, dtype=jnp.int32)
    live_mask = (ordinal[None, :] < live_rows[:, None]).astype(jnp.float32)
    masked_factor = inverse_factor * live_mask[:, :, None] * live_mask[:, None, :]
    turned_rows = jnp.transpose(
        block_rows.reshape(blocks, padded, groups, NPAN, window), (0, 1, 3, 2, 4)
    ).reshape(blocks, padded, NPAN * lanes)
    whitened = jnp.einsum(
        "bij,bjm->bim",
        masked_factor,
        turned_rows.astype(jnp.float32),
        precision=lax.Precision.HIGHEST,
    ).astype(jnp.bfloat16).reshape(depth, NPAN * lanes)

    part_0 = lax.reduce_precision(shift[:window], 8, 7)
    rest = shift[:window] - part_0
    part_1 = lax.reduce_precision(rest, 8, 7)
    parts = jnp.stack([part_0, part_1, rest - part_1], axis=1).astype(jnp.bfloat16)
    own_block = jnp.arange(groups, dtype=jnp.int32)[:, None, None] == own_g
    spare = jnp.where(own_block, parts[None], 0.0).astype(jnp.bfloat16).reshape(lanes, 3)
    turned = whitened.T
    panel_t = jnp.concatenate(
        [turned[:lanes], spare, jnp.zeros((lanes, wide - depth - 3), jnp.bfloat16)], axis=1
    )

    half = lanes // 2
    first = panel_t[:half]
    first = jnp.stack([first, swap(first, "grp", 2)])
    first = jnp.concatenate([first, swap(first, "col", 1)])
    second = panel_t[half:]
    second = jnp.stack([second] + [turn(second, "row", k) for k in range(1, rowcount)])
    second = jnp.concatenate([second, swap(second, "col", 1)])
    firsts = [first] + [turn(first, "row", k) for k in range(1, rowcount)]
    seconds = [second, swap(second, "grp", 2)]
    pieces = (
        firsts
        + [swap(x, "grp", 1) for x in firsts]
        + seconds
        + [swap(x, "grp", 1) for x in seconds]
    )

    whole = lax.all_gather(whitened[:, lanes:], ("grp", "row"), axis=0, tiled=False)
    whole = whole.reshape(groups, rowcount, depth, (NPAN - 1) * lanes)

    row_pieces = jnp.transpose(turned.reshape(NPAN, groups, window, depth), (1, 0, 2, 3))
    row_pieces = jnp.pad(
        row_pieces.reshape(groups, NPAN * window, depth), ((0, 0), (0, 0), (0, wide - depth))
    )
    row_pieces, _ = lax.optimization_barrier((row_pieces, firsts[1]))
    rows_in = []
    for k in range(groups):
        piece = lax.dynamic_index_in_dim(row_pieces, own_g ^ k, 0, keepdims=False)
        rows_in.append(swap(piece, "grp", k) if k else piece)
    rows_in = rows_in + [swap(x, "col", 1) for x in rows_in]

    panel, inverse = panel_inverse(place, pieces, depth)
    panel_piece, v_t = rows_update(place, panel, inverse, rows_in, depth, local_rows)

    tile = owners * window
    own_cols = jnp.arange(tile, dtype=jnp.int32)
    diag = jnp.where(
        own_cols[None, None, :]
        == (own_g * rowcount + own_r) * window
        + jnp.arange(window, dtype=jnp.int32)[None, :, None],
        shift.reshape(NPAN, window, 1),
        0.0,
    )
    return trailing(place, v_t, panel_piece, whole, diag)


def solution(mesh):
    in_specs = (
        P("grp", None, ("row", "col")),
        P("grp", None, None),
        P("grp"),
        P(("grp", "row", "col")),
    )
    out_specs = P(("grp", "row"), "col")
    return jax.shard_map(local, mesh=mesh, in_specs=in_specs, out_specs=out_specs, check_vma=False)
```
